32 devices in a mesh: row: 4 (over x, core), col: 8 (over z, y).
Axes of the slice: x: 2, y: 2, z: 4, core: 2. Of those that a mesh axis runs over, the one named last changes fastest.
Arguments:
- covariates: float32 [16, 8192], P(None, ('row', 'col')), may hold values from -6 to 6
- lengthscale: float32 [16], replicated, may hold values from 1 to 3
- nugget: float32 [8192], P(('row', 'col')), may hold values from 0.5 to 2
- patch_values: bfloat16 [8192, 16, 128], P(('row', 'col')), may hold values from -6 to 6
- patch_weights: bfloat16 [8192, 8, 128], P(('row', 'col')), may hold values from 0 to 0.1796875
- block_index: int32 [8192, 8], P(('row', 'col')), may hold values from 0 to 255
- slot_count: int32 [8192], P(('row', 'col')), may hold values from 1 to 8
- owner: int32 [8192, 1], P(('row', 'col')), may hold values from 0 to 31; in each aligned block of 256 rows (0 to 255, 256 to 511, ...) at most 16 rows name the same one
Outputs:
- solution: float32 [16, 8192], P(None, ('row', 'col'))
- residual: float32 [16, 8192], P(None, ('row', 'col'))
The draws below stay inside these ranges and needn't reach their ends.
Inputs may be any that keep to these rules, and one draw needn't show every extreme that they name: Among the 256 patches held by one device, no owner is named more than 16 times.
All inputs are finite; a program needn't handle non-finite values.
Results may differ from the reference program's by a relative error of at most 0.00045.
Values may be sent and summed in bfloat16 or wider, within the bound.
A program may use at most 64 MiB of HBM per device.

```python
import math
import jax
import jax.numpy as jnp
import numpy as np
from jax import lax

FEATS = 16
MEMBERS = 16
CELLS = 128
SLOTS = 8
ST_DEV = 256
PATCH_DEV = 256
ITERS = 2
STATIONS = 8192
PATCHES = 8192
CAP = 16
DEVICES = 32


def touch_ends(array, stream_key, smallest, high):
    place = [jax.random.randint(jax.random.fold_in(stream_key, axis), (), 0, length) for axis, length in enumerate(array.shape)]
    widest = array.shape.index(max(array.shape))
    beside = place[:widest] + [(place[widest] + 1) % array.shape[widest]] + place[widest + 1:]
    return array.at[tuple(place)].set(smallest).at[tuple(beside)].set(high)


def steps_of(key, extent, shards, low, high):
    gain = 1.0
    for dim, parts in shards:
        steps = jax.random.uniform(jax.random.fold_in(jax.random.fold_in(key, 6), dim), (parts,), jnp.float32, low / len(shards), high / len(shards))
        gain = gain * jnp.repeat(jnp.exp(steps), extent[dim] // parts).reshape((-1,) + (1,) * (len(extent) - 1 - dim))
    return gain


def assign_block(key, own, number, rows, count, top, bound, skew):
    ranking = jax.random.permutation(key, count)
    crowded, common = portions_of(count, rows * top, bound, skew, True), portions_of(count, rows * top, bound, skew, False)
    places = jnp.arange(count)

    def named(lengths, turn):
        used = int((lengths > 0).sum())
        fixed = max(1, used // 4)
        passed = fixed + (places - fixed + turn * (used - fixed)) % max(1, count - fixed)
        return jnp.zeros((count,), jnp.int32).at[ranking[jnp.where(places < fixed, places, passed)]].set(jnp.asarray(lengths, jnp.int32))

    lengths = jnp.where(number % 4 == 0, named(crowded, number // 4), named(common, number - number // 4 - 1))
    mixed = jax.random.permutation(jax.random.fold_in(own, 3), count)
    giver, receiver = mixed[0:count // 2 * 2:2], mixed[1:count // 2 * 2:2]
    room = jnp.minimum(lengths[giver] - 1, bound - lengths[receiver]) // 2
    room = jnp.where((giver == ranking[0]) | (receiver == ranking[0]) | (lengths[receiver] == 0), 0, jnp.maximum(room, 0))
    passed = jax.random.randint(jax.random.fold_in(own, 4), (count // 2,), 0, 1 << 20) % (room + 1)
    lengths = lengths.at[giver].add(-passed).at[receiver].add(passed)
    labels = jnp.searchsorted(jnp.cumsum(lengths), jnp.arange(rows * top), side="right").astype(jnp.int32)
    grid = labels.reshape(top, rows).T
    grid = grid[jax.random.permutation(jax.random.fold_in(own, 1), rows)]
    turn = jax.random.randint(jax.random.fold_in(own, 2), (rows, 1), 0, top)
    return jnp.take_along_axis(grid, (jnp.arange(top)[None, :] + turn) % top, axis=1)


def portions_of(count, total, limit, skew, full):
    portions = [(1 << 20) // math.isqrt(standing ** skew) + 1 for standing in range(1, count + 1)]
    largest = limit if full else min(limit, max(-(-total // count), total * portions[0] // sum(portions)))
    least = 1 if total - largest >= count - 1 else 0
    given, surplus = [largest] + [least] * (count - 1), total - largest - least * (count - 1)
    while surplus > 0:
        movable = [i for i in range(1, count) if given[i] < largest] or [i for i in range(1, count) if given[i] < limit]
        whole, left = sum([portions[i] for i in movable]), surplus
        for i in movable:
            more = min(limit - given[i], max(1, left * portions[i] // whole), surplus)
            given[i] = given[i] + more
            surplus = surplus - more
    return np.array(given)


def gaussian(stream_key, extent, deviation, limit, pieces=(), held_as=jnp.bfloat16):
    drawn = deviation * jax.random.normal(stream_key, extent, jnp.float32)
    if pieces:
        drawn = drawn * steps_of(stream_key, extent, pieces, -0.22, 0.18)
    return jnp.clip(drawn, -limit, limit).astype(held_as)


def setup_inputs(seed: int = 0) -> dict:
    seeds = jax.random.split(jax.random.key(seed), 9)
    covariates = gaussian(seeds[0], (FEATS, STATIONS), 1.0, 6.0, ((1, 32),), jnp.float32)
    lengthscale = jnp.clip(jnp.exp(jax.random.uniform(seeds[1], (FEATS,), jnp.float32, math.log(1.0), math.log(3.0))), 1.0, 3.0)
    nugget = jnp.clip(jnp.exp(math.log(2.0) - 1.3862944 * jax.random.uniform(seeds[2], (STATIONS,), jnp.float32) ** steps_of(seeds[2], (STATIONS,), ((0, 32),), -0.2, 0.2)), 0.5, 2.0)
    patch_values = gaussian(seeds[3], (PATCHES, MEMBERS, CELLS), 1.0, 6.0, ((0, 32),))
    patch_weights = jnp.clip(0.1796875 * jax.random.uniform(seeds[4], (PATCHES, SLOTS, CELLS), jnp.float32) ** steps_of(seeds[4], (PATCHES, SLOTS, CELLS), ((0, 32),), -0.2, 0.2), 0.0, 0.1796875).astype(jnp.bfloat16)
    block_index = touch_ends(jax.random.randint(seeds[5], (PATCHES, SLOTS), 0, ST_DEV), jax.random.fold_in(seeds[5], 1), 0, ST_DEV - 1).astype(jnp.int32)
    slot_count = touch_ends(jax.random.randint(seeds[6], (PATCHES,), 1, SLOTS + 1), jax.random.fold_in(seeds[6], 1), 1, SLOTS).astype(jnp.int32)
    owner_keys = jax.random.split(jax.random.fold_in(seeds[7], 1), PATCHES // PATCH_DEV)
    owner_turns = jax.random.permutation(jax.random.fold_in(seeds[7], 3), PATCHES // PATCH_DEV)
    owner = jax.vmap(lambda own, number: assign_block(jax.random.fold_in(seeds[7], 2), own, number, PATCH_DEV, DEVICES, 1, CAP, 2))(owner_keys, owner_turns).reshape((PATCHES, 1))
    return dict(covariates=covariates, lengthscale=lengthscale, nugget=nugget, patch_values=patch_values, patch_weights=patch_weights, block_index=block_index, slot_count=slot_count, owner=owner)


ROOT_FIVE = 5.0 ** 0.5
HIGH = lax.Precision.HIGHEST

def matern(left, right):
    cross = lax.dot_general(left, right, (((0,), (0,)), ((), ())), precision=HIGH, preferred_element_type=jnp.float32)
    squared = lax.optimization_barrier(jnp.sum(left * left, axis=0))[:, None] + lax.optimization_barrier(jnp.sum(right * right, axis=0))[None, :] - 2.0 * cross
    scaled = ROOT_FIVE * jnp.sqrt(jnp.maximum(squared, 0.0))
    return (1.0 + scaled + scaled * scaled / 3.0) * jnp.exp(-scaled)

def apply_operator(direction, scaled_cov, nugget):
    width = math.gcd(STATIONS, 1024)
    count = STATIONS // width
    column_sets = jnp.transpose(scaled_cov.reshape(scaled_cov.shape[0], count, width), (1, 0, 2))

    def one_block(block_cov):
        return jnp.dot(direction, matern(scaled_cov, block_cov), precision=HIGH, preferred_element_type=jnp.float32)
    images = lax.map(one_block, column_sets)
    image = jnp.transpose(images, (1, 0, 2)).reshape(direction.shape[0], STATIONS)
    return image + nugget[None, :] * direction

def reference(covariates, lengthscale, nugget, patch_values, patch_weights, block_index, slot_count, owner):
    terms = jnp.einsum('psc,pmc->pms', patch_weights.astype(jnp.float32), patch_values.astype(jnp.float32))
    live = (jnp.arange(SLOTS, dtype=jnp.int32)[None, :] < slot_count[:, None]).astype(jnp.float32)
    terms = terms * live[:, None, :]
    station = (owner[:, 0][:, None] * ST_DEV + block_index).astype(jnp.int32)
    flat = jnp.transpose(terms, (0, 2, 1)).reshape(-1, MEMBERS)
    rhs = jax.ops.segment_sum(flat, station.reshape(-1), num_segments=STATIONS).T
    scaled_cov = covariates / lengthscale[:, None]
    solution = jnp.zeros_like(rhs)
    residual = rhs
    direction = rhs
    norm_now = lax.optimization_barrier(jnp.sum(residual * residual, axis=1))
    for step in range(ITERS):
        image = apply_operator(direction, scaled_cov, nugget)
        alpha = norm_now / lax.optimization_barrier(jnp.sum(direction * image, axis=1))
        solution = solution + alpha[:, None] * direction
        residual = residual - alpha[:, None] * image
        norm_next = lax.optimization_barrier(jnp.sum(residual * residual, axis=1))
        direction = residual + (norm_next / norm_now)[:, None] * direction
        norm_now = norm_next
    return (solution, residual)
```

```python
import functools
import math

import jax
import jax.numpy as jnp
from jax import lax
from jax.experimental import pallas as pl
from jax.experimental.pallas import tpu as pltpu
from jax.sharding import PartitionSpec as P

MESH = pl.DeviceIdType.MESH
F32, BF16 = jnp.float32, jnp.bfloat16
LOG2E = 1.0 / math.log(2.0)
SCALE = 5.0 * LOG2E * LOG2E
LINEAR = math.log(2.0)
SQUARE = math.log(2.0) ** 2 / 3.0


def iota(shape, axis):
    return lax.broadcasted_iota(jnp.int32, shape, axis)


def mm(a, b):
    return jnp.dot(a, b, preferred_element_type=F32)


def mm_nt(a, b):
    return lax.dot_general(a, b, (((1,), (1,)), ((), ())), preferred_element_type=F32)


def split2(x):
    hi = x.astype(BF16)
    return hi, (x - hi.astype(F32)).astype(BF16)


def split3(x):
    hi = x.astype(BF16).astype(F32)
    rest = x - hi
    mid = rest.astype(BF16).astype(F32)
    return hi, mid, rest - mid


def stack(parts, rows):
    place = iota((rows, parts[0].shape[1]), 0)
    out = jnp.zeros((rows, parts[0].shape[1]), F32)
    for number, part in enumerate(parts):
        out = jnp.where(place == number, part, out)
    return out


def features(z, left):
    feats, width = z.shape
    norm = split3(SCALE * jnp.sum(z * z, axis=0, keepdims=True))
    ones = [jnp.ones((1, width), F32)] * 3
    hi, mid, low = split3(z * (-2.0 * SCALE)) if left else split3(z)
    if left:
        parts, tail = [hi, hi, mid, mid, hi, low], list(norm) + ones
    else:
        parts, tail = [hi, mid, hi, mid, low, hi], ones + list(norm)
    used = 6 * feats + 8
    padded = -(-used // 128) * 128
    parts = parts + [stack(tail, 8)]
    if padded > used:
        parts.append(jnp.zeros((padded - used, width), F32))
    return jnp.concatenate(parts, axis=0)


def kernel(
    rows, cols, cap,
    cov, ls, nug, val, wts, idx, cnt, own,
    sol, res,
    zrow, zcol, left, right, k_hi, k_lo,
    tsend, trecv, isend, irecv, vrow, vcol, pout, pin, scal,
    zr_s, zr_r, zc_s, zc_r, t_s, t_r, i_s, i_r,
    vr_s, vr_r, vc_s, vc_r, p_s, p_r, s_s, s_r,
):
    devices = rows * cols
    r, c = lax.axis_index("row"), lax.axis_index("col")
    me = r * cols + c
    feats, st = cov.shape
    held, slots = idx.shape
    members = val.shape[0] // held
    group = 128 // slots

    def place(k):
        other = lax.rem(me + k, devices)
        return other, (lax.div(other, cols), lax.rem(other, cols))

    barrier = pltpu.get_barrier_semaphore()

    def greet(k, carry):
        pl.semaphore_signal(barrier, inc=1, device_id=place(k)[1], device_id_type=MESH)
        return carry

    lax.fori_loop(1, devices, greet, 0)

    def row_copy(buf, ss, rs, k, slot):
        other = lax.rem(r + k, rows)
        at = r if slot is None else other
        return pltpu.make_async_remote_copy(
            src_ref=buf.at[at], dst_ref=buf.at[at], send_sem=ss.at[other], recv_sem=rs.at[at],
            device_id=(other, c), device_id_type=MESH)

    def col_copy(src, buf, ss, rs, k, slot):
        other = lax.rem(c + k, cols)
        at = c if slot is None else other
        return pltpu.make_async_remote_copy(
            src_ref=src.at[other] if src is not buf else buf.at[at], dst_ref=buf.at[at],
            send_sem=ss.at[other], recv_sem=rs.at[at],
            device_id=(r, other), device_id_type=MESH)

    def all_copy(src, buf, ss, rs, k, slot):
        other, where = place(k)
        at = me if slot is None else other
        return pltpu.make_async_remote_copy(
            src_ref=src.at[other] if src is not buf else buf.at[at], dst_ref=buf.at[at],
            send_sem=ss.at[other], recv_sem=rs.at[at],
            device_id=where, device_id_type=MESH)

    def each(count, act):
        def step(k, carry):
            act(k)
            return carry
        lax.fori_loop(1, count, step, 0)

    diag = iota((feats, feats), 0) == iota((feats, feats), 1)
    scale = jnp.sum(jnp.where(diag, ls[...], 0.0), axis=1, keepdims=True)
    z = cov[...] / scale
    zrow[r] = z
    zcol[c] = z

    eye = iota((held, held), 0) == iota((held, held), 1)
    own_col = own[...].astype(F32)
    own_row = jnp.sum(jnp.where(eye, own_col, 0.0), axis=0, keepdims=True)
    cnt_col = jnp.sum(jnp.where(eye, cnt[...].astype(F32), 0.0), axis=1, keepdims=True)
    same = (own_col == own_row) & (iota((held, held), 1) < iota((held, held), 0))
    rank = jnp.sum(jnp.where(same, 1.0, 0.0), axis=1, keepdims=True)
    position = own_col * cap + rank

    live = iota((held, slots), 1).astype(F32) < cnt_col
    station = jnp.where(live, idx[...].astype(F32), float(st))
    spread = jnp.where(iota((slots, 128), 1) % slots == iota((slots, 128), 0), 1.0, 0.0)
    wide = mm(station.astype(BF16), spread.astype(BF16))
    wide = jnp.where((iota((held, 128), 1) // slots).astype(F32) == rank, wide, 0.0)
    to_owner = jnp.where(iota((devices, held), 0).astype(F32) == own_row, 1.0, 0.0)
    index_rows = mm(to_owner.astype(BF16), wide.astype(BF16))
    for o in range(devices):
        isend[o] = index_rows[o : o + 1]

    blocks = iota((group, members, 128), 0) == iota((group, members, 128), 2) // slots
    lane_patch = iota((group, 128), 1) // slots == iota((group, 128), 0)
    slot_of = iota((members, 128), 1) % slots
    total = jnp.zeros((devices * cap, 2 * slots * members), F32)
    tables, spreads = [], []
    for g in range(held // group):
        cross = mm_nt(
            val[g * group * members : (g + 1) * group * members, :],
            wts[g * 128 : (g + 1) * 128, :],
        ).reshape(group, members, 128)
        terms = jnp.sum(jnp.where(blocks, cross, 0.0), axis=0)
        hi = terms.astype(BF16).astype(F32)
        low = terms - hi
        by_slot = [jnp.where(slot_of == s, part, 0.0) for part in (hi, low) for s in range(slots)]
        spreads.append(jnp.concatenate(by_slot, axis=0).astype(BF16))
        at = jnp.sum(
            jnp.where(lane_patch, position[g * group : (g + 1) * group], 0.0), axis=0, keepdims=True)
        tables.append(
            jnp.where(iota((devices * cap, 128), 0).astype(F32) == at, 1.0, 0.0).astype(BF16))
        if len(tables) == 4 or g + 1 == held // group:
            total = total + mm_nt(jnp.concatenate(tables, axis=1), jnp.concatenate(spreads, axis=1))
            tables, spreads = [], []
    packed = total[:, : slots * members] + total[:, slots * members :]
    tsend[...] = packed.reshape(devices, cap, slots * members)
    trecv[me] = tsend[me]
    irecv[me] = isend[me]

    pl.semaphore_wait(barrier, devices - 1)
    each(rows, lambda k: row_copy(zrow, zr_s, zr_r, k, None).start())
    each(cols, lambda k: col_copy(zcol, zcol, zc_s, zc_r, k, None).start())

    def send_terms(k):
        all_copy(tsend, trecv, t_s, t_r, k, None).start()
        all_copy(isend, irecv, i_s, i_r, k, None).start()

    each(devices, send_terms)

    each(rows, lambda k: row_copy(zrow, zr_s, zr_r, k, 1).wait_recv())
    for i in range(rows):
        left[i * st : (i + 1) * st, :] = features(zrow[i], True).T.astype(BF16)
    each(cols, lambda k: col_copy(zcol, zcol, zc_s, zc_r, k, 1).wait_recv())

    def make_right(i, carry):
        right[i] = features(zcol[i], False).astype(BF16)
        return carry

    lax.fori_loop(0, cols, make_right, 0)

    chunk = 128
    chunks = rows * st // chunk

    def make_kernel(t, carry):
        j, i = lax.div(t, chunks), lax.rem(t, chunks)
        here = pl.ds(pl.multiple_of(i * chunk, chunk), chunk)
        square = jnp.maximum(mm(left[here, :], right[j]), 1e-30)
        w = square * lax.rsqrt(square)
        value = (1.0 + LINEAR * w + SQUARE * square) * jnp.exp2(-w)
        hi, low = split2(value)
        k_hi[j, here, :] = hi
        k_lo[j, here, :] = low
        return carry

    lax.fori_loop(0, cols * chunks, make_kernel, 0)

    def wait_terms(k):
        all_copy(tsend, trecv, t_s, t_r, k, 1).wait_recv()
        all_copy(isend, irecv, i_s, i_r, k, 1).wait_recv()

    each(devices, wait_terms)
    got = devices * cap
    rep = jnp.where(iota((got, devices), 0) // cap == iota((got, devices), 1), 1.0, 0.0)
    seen = irecv[...].reshape(devices, 128)
    z_rows = mm(rep.astype(BF16), seen.astype(BF16))
    z_rows = jnp.where(iota((got, 128), 0) % cap == iota((got, 128), 1) // slots, z_rows, 0.0)
    by_slot = mm_nt(spread.astype(BF16), z_rows.astype(BF16))
    flat = trecv[...].reshape(got, slots * members).T
    names = iota((st, got), 0).astype(F32)
    rhs2 = jnp.zeros((2 * members, st), F32)
    for s in range(slots):
        hi, low = split2(flat[s * members : (s + 1) * members])
        hit = jnp.where(names == by_slot[s : s + 1], 1.0, 0.0).astype(BF16)
        rhs2 = rhs2 + mm_nt(jnp.concatenate([hi, low], axis=0), hit)
    rhs = rhs2[:members] + rhs2[members:]

    lane, sub = iota((members, 128), 1), iota((members, 128), 0)

    def operate(turn, v):
        vr, vc = vrow.at[turn], vcol.at[turn]
        vr[r] = v
        vc[c] = v
        each(rows, lambda k: row_copy(vr, vr_s.at[turn], vr_r.at[turn], k, None).start())
        each(cols, lambda k: col_copy(vc, vc, vc_s.at[turn], vc_r.at[turn], k, None).start())
        each(rows, lambda k: row_copy(vr, vr_s.at[turn], vr_r.at[turn], k, 1).wait_recv())
        whole = jnp.concatenate([vr[i] for i in range(rows)], axis=1)
        hi, low = split2(whole)
        both = jnp.concatenate([hi, low], axis=0)
        each(cols, lambda k: col_copy(vc, vc, vc_s.at[turn], vc_r.at[turn], k, 1).wait_recv())

        def part(other):
            double = mm(both, k_hi[other])
            return double[:members] + double[members:] + mm(hi, k_lo[other])

        def one(k, acc):
            other = lax.rem(c + k, cols)
            mine = part(other)
            pout[turn, other] = mine
            col_copy(pout.at[turn], pin.at[turn], p_s.at[turn], p_r.at[turn], k, None).start()
            return acc + mine * vc[other]

        acc = lax.fori_loop(1, cols, one, jnp.zeros((members, st), F32))
        mine = part(c)
        pin[turn, c] = mine
        shift = nug[...] * v
        acc = acc + (mine + shift) * v
        norm = jnp.sum(v * v, axis=1, keepdims=True)
        product = jnp.sum(acc, axis=1, keepdims=True)
        line = jnp.where(lane == sub, norm, 0.0) + jnp.where(lane == sub + members, product, 0.0)
        sc = scal.at[turn]
        sc[me] = jnp.sum(line, axis=0, keepdims=True)
        each(devices, lambda k: all_copy(sc, sc, s_s.at[turn], s_r.at[turn], k, None).start())
        each(cols, lambda k: col_copy(
            pout.at[turn], pin.at[turn], p_s.at[turn], p_r.at[turn], k, 1).wait_recv())
        image = shift + jnp.sum(pin[turn], axis=0)
        each(devices, lambda k: all_copy(sc, sc, s_s.at[turn], s_r.at[turn], k, 1).wait_recv())
        sums = jnp.sum(sc[...], axis=0)
        norm = jnp.sum(jnp.where(lane == sub, sums, 0.0), axis=1, keepdims=True)
        product = jnp.sum(jnp.where(lane == sub + members, sums, 0.0), axis=1, keepdims=True)
        return image, norm, product

    image, norm, product = operate(0, rhs)
    alpha = norm / product
    residual = rhs - alpha * image
    image_next, norm_next, product = operate(1, residual)
    ratio = norm_next / norm
    alpha_next = norm_next / (product - ratio * norm_next / alpha)
    sol[...] = alpha * rhs + alpha_next * (residual + ratio * rhs)
    res[...] = residual - alpha_next * (image_next + ratio * image)

    each(rows, lambda k: row_copy(zrow, zr_s, zr_r, k, 1).wait_send())
    each(cols, lambda k: col_copy(zcol, zcol, zc_s, zc_r, k, 1).wait_send())

    def sent(k):
        all_copy(tsend, trecv, t_s, t_r, k, 1).wait_send()
        all_copy(isend, irecv, i_s, i_r, k, 1).wait_send()
        for turn in range(2):
            sc = scal.at[turn]
            all_copy(sc, sc, s_s.at[turn], s_r.at[turn], k, 1).wait_send()

    each(devices, sent)
    for turn in range(2):
        vr, vc = vrow.at[turn], vcol.at[turn]
        each(rows, lambda k: row_copy(vr, vr_s.at[turn], vr_r.at[turn], k, 1).wait_send())
        each(cols, lambda k: col_copy(vc, vc, vc_s.at[turn], vc_r.at[turn], k, 1).wait_send())
        each(cols, lambda k: col_copy(
            pout.at[turn], pin.at[turn], p_s.at[turn], p_r.at[turn], k, 1).wait_send())


def local(rows, cols, covariates, lengthscale, nugget, patch_values, patch_weights, block_index,
          slot_count, owner):
    devices = rows * cols
    feats, st = covariates.shape
    held, members, cells = patch_values.shape
    slots = patch_weights.shape[1]
    cap = max(128 // slots, 2 * held // devices)
    wide = -(-(6 * feats + 8) // 128) * 128
    dma = pltpu.SemaphoreType.DMA
    vmem = pltpu.VMEM
    scratch = [
        vmem((rows, feats, st), F32),
        vmem((cols, feats, st), F32),
        vmem((rows * st, wide), BF16),
        vmem((cols, wide, st), BF16),
        vmem((cols, rows * st, st), BF16),
        vmem((cols, rows * st, st), BF16),
        vmem((devices, cap, slots * members), F32),
        vmem((devices, cap, slots * members), F32),
        vmem((devices, 1, 128), F32),
        vmem((devices, 1, 128), F32),
        vmem((2, rows, members, st), F32),
        vmem((2, cols, members, st), F32),
        vmem((2, cols, members, st), F32),
        vmem((2, cols, members, st), F32),
        vmem((2, devices, 1, 128), F32),
    ]
    sems = [(rows,)] * 2 + [(cols,)] * 2 + [(devices,)] * 4
    sems += [(2, rows)] * 2 + [(2, cols)] * 4 + [(2, devices)] * 2
    scratch += [dma(shape) for shape in sems]
    spec = pl.BlockSpec(memory_space=pltpu.VMEM)
    return pl.pallas_call(
        functools.partial(kernel, rows, cols, cap),
        out_shape=[jax.ShapeDtypeStruct((members, st), F32)] * 2,
        in_specs=[spec] * 8,
        out_specs=[spec] * 2,
        scratch_shapes=scratch,
        compiler_params=pltpu.CompilerParams(
            collective_id=0, has_side_effects=True, vmem_limit_bytes=56 * 2**20),
    )(
        covariates,
        lengthscale.reshape(1, feats),
        nugget.reshape(1, st),
        patch_values.reshape(held * members, cells),
        patch_weights.reshape(held * slots, cells),
        block_index,
        slot_count.reshape(1, held),
        owner,
    )


def solution(mesh):
    placed = (
        P(None, ("row", "col")),
        P(),
        P(("row", "col")),
        P(("row", "col"), None, None),
        P(("row", "col"), None, None),
        P(("row", "col"), None),
        P(("row", "col")),
        P(("row", "col"), None),
    )
    return jax.shard_map(
        functools.partial(local, mesh.shape["row"], mesh.shape["col"]),
        mesh=mesh,
        in_specs=placed,
        out_specs=(P(None, ("row", "col")), P(None, ("row", "col"))),
        check_vma=False,
    )
```

```python
import functools
import math

import jax
import jax.numpy as jnp
from jax import lax
from jax.experimental import pallas as pl
from jax.experimental.pallas import tpu as pltpu
from jax.sharding import PartitionSpec as P

MESH = pl.DeviceIdType.MESH
F32, BF16 = jnp.float32, jnp.bfloat16
LOG2E = 1.0 / math.log(2.0)
SCALE = 5.0 * LOG2E * LOG2E
LINEAR = math.log(2.0)
SQUARE = math.log(2.0) ** 2 / 3.0


def iota(shape, axis):
    return lax.broadcasted_iota(jnp.int32, shape, axis)


def mm(a, b):
    return jnp.dot(a, b, preferred_element_type=F32)


def mm_nt(a, b):
    return lax.dot_general(a, b, (((1,), (1,)), ((), ())), preferred_element_type=F32)


def split2(x):
    hi = x.astype(BF16)
    return hi, (x - hi.astype(F32)).astype(BF16)


def split3(x):
    hi = x.astype(BF16).astype(F32)
    rest = x - hi
    mid = rest.astype(BF16).astype(F32)
    return hi, mid, rest - mid


def stack(parts, rows):
    place = iota((rows, parts[0].shape[1]), 0)
    out = jnp.zeros((rows, parts[0].shape[1]), F32)
    for number, part in enumerate(parts):
        out = jnp.where(place == number, part, out)
    return out


def features(z, left):
    feats, width = z.shape
    norm = split3(SCALE * jnp.sum(z * z, axis=0, keepdims=True))
    ones = [jnp.ones((1, width), F32)] * 3
    hi, mid, low = split3(z * (-2.0 * SCALE)) if left else split3(z)
    if left:
        parts, tail = [hi, hi, mid, mid, hi, low], list(norm) + ones
    else:
        parts, tail = [hi, mid, hi, mid, low, hi], ones + list(norm)
    used = 6 * feats + 8
    padded = -(-used // 128) * 128
    parts = parts + [stack(tail, 8)]
    if padded > used:
        parts.append(jnp.zeros((padded - used, width), F32))
    return jnp.concatenate(parts, axis=0)


def kernel(
    rows, cols, cap,
    cov, ls, nug, val_hbm, wts_hbm, idx, cnt, own,
    out,
    val, wts, zrow, zcol, left, right, k_hi, k_lo,
    tsend, trecv, isend, irecv, vrow, vcol, base, pout, pin, scal,
    load, zr_s, zr_r, zc_s, zc_r, t_s, t_r, i_s, i_r,
    vr_s, vr_r, vc_s, vc_r, p_s, p_r, s_s, s_r,
):
    devices = rows * cols
    r, c = lax.axis_index("row"), lax.axis_index("col")
    me = r * cols + c
    feats, st = cov.shape
    slots, held = idx.shape
    members = val.shape[0] // held
    group = 128 // slots

    def row_of(k):
        return jnp.where(r + k >= rows, r + k - rows, r + k)

    def col_of(k):
        return jnp.where(c + k >= cols, c + k - cols, c + k)

    around = [col_of(k) for k in range(cols)]

    def to_all(act):
        for k in range(1, cols):
            act(r * cols + around[k], (r, around[k]))

        def step(k, carry):
            other = row_of(k)
            for column in around:
                act(other * cols + column, (other, column))
            return carry

        lax.fori_loop(1, rows, step, 0)

    def to_row(act):
        for k in range(1, rows):
            act(row_of(k), (row_of(k), c))

    def to_col(act):
        for k in range(1, cols):
            act(around[k], (r, around[k]))

    def push(src, dst, ss, rs, where):
        pltpu.make_async_remote_copy(
            src_ref=src, dst_ref=dst, send_sem=ss, recv_sem=rs,
            device_id=where, device_id_type=MESH).start()

    def await_all(buf, sem):
        part = buf.at[pl.ds(0, buf.shape[0] - 1)]
        pltpu.make_async_copy(part, part, sem).wait()

    loads = [pltpu.make_async_copy(val_hbm, val, load.at[0]),
             pltpu.make_async_copy(wts_hbm, wts, load.at[1])]
    for copy in loads:
        copy.start()

    barrier = pltpu.get_barrier_semaphore()
    to_all(lambda other, where: pl.semaphore_signal(
        barrier, inc=1, device_id=where, device_id_type=MESH))

    diag = iota((feats, feats), 0) == iota((feats, feats), 1)
    scale = jnp.sum(jnp.where(diag, ls[...], 0.0), axis=1, keepdims=True)
    z = cov[...] / scale
    zrow[r] = z
    zcol[c] = z

    eye = iota((held, held), 0) == iota((held, held), 1)
    own_row = own[...].astype(F32)
    own_col = jnp.sum(jnp.where(eye, own_row, 0.0), axis=1, keepdims=True)
    same = (own_col == own_row) & (iota((held, held), 1) < iota((held, held), 0))
    rank = jnp.sum(jnp.where(same, 1.0, 0.0), axis=1, keepdims=True)
    position = own_col * cap + rank

    live = iota((slots, held), 0) < cnt[...]
    station = jnp.where(live, idx[...].astype(F32), float(st))
    station = jnp.concatenate([station, jnp.zeros((128 - slots, held), F32)], axis=0).T
    spread = jnp.where(iota((128, 128), 1) % slots == iota((128, 128), 0), 1.0, 0.0)
    wide = mm(station.astype(BF16), spread.astype(BF16))
    wide = jnp.where((iota((held, 128), 1) // slots).astype(F32) == rank, wide, 0.0)
    to_owner = jnp.where(iota((devices, held), 0).astype(F32) == own_row, 1.0, 0.0)
    index_rows = mm(to_owner.astype(BF16), wide.astype(BF16))
    for o in range(devices):
        isend[o] = index_rows[o : o + 1]
    irecv[me] = isend[me]

    pl.semaphore_wait(barrier, devices - 1)
    to_row(lambda other, where: push(zrow.at[r], zrow.at[r], zr_s, zr_r, where))
    to_col(lambda other, where: push(zcol.at[c], zcol.at[c], zc_s, zc_r, where))

    for copy in loads:
        copy.wait()
    blocks = iota((group, members, 128), 0) == iota((group, members, 128), 2) // slots
    lane_patch = iota((group, 128), 1) // slots == iota((group, 128), 0)
    slot_of = iota((members, 128), 1) % slots
    total = jnp.zeros((devices * cap, 2 * slots * members), F32)
    tables, spreads = [], []
    for g in range(held // group):
        cross = mm_nt(
            val[g * group * members : (g + 1) * group * members, :],
            wts[g * 128 : (g + 1) * 128, :],
        ).reshape(group, members, 128)
        terms = jnp.sum(jnp.where(blocks, cross, 0.0), axis=0)
        hi = terms.astype(BF16).astype(F32)
        low = terms - hi
        by_slot = [jnp.where(slot_of == s, part, 0.0) for part in (hi, low) for s in range(slots)]
        spreads.append(jnp.concatenate(by_slot, axis=0).astype(BF16))
        at = jnp.sum(
            jnp.where(lane_patch, position[g * group : (g + 1) * group], 0.0), axis=0, keepdims=True)
        tables.append(
            jnp.where(iota((devices * cap, 128), 0).astype(F32) == at, 1.0, 0.0).astype(BF16))
        if len(tables) == 4 or g + 1 == held // group:
            total = total + mm_nt(jnp.concatenate(tables, axis=1), jnp.concatenate(spreads, axis=1))
            tables, spreads = [], []
    packed = total[:, : slots * members] + total[:, slots * members :]
    tsend[...] = packed.reshape(devices, cap, slots * members)
    trecv[me] = tsend[me]

    def send_terms(other, where):
        push(tsend.at[other], trecv.at[me], t_s, t_r, where)
        push(isend.at[other], irecv.at[me], i_s, i_r, where)

    to_all(send_terms)

    await_all(zrow, zr_r)
    for k in range(rows):
        left[k * st : (k + 1) * st, :] = features(zrow[row_of(k)], True).T.astype(BF16)
    await_all(zcol, zc_r)

    def make_right(k, carry):
        right[k] = features(zcol[col_of(k)], False).astype(BF16)
        return carry

    lax.fori_loop(0, cols, make_right, 0)

    chunk = 2 * st
    chunks = rows * st // chunk

    def make_kernel(j, carry):
        for i in range(chunks):
            here = pl.ds(i * chunk, chunk)
            square = jnp.maximum(mm(left[here, :], right[j]), 1e-30)
            w = square * lax.rsqrt(square)
            value = (1.0 + LINEAR * w + SQUARE * square) * jnp.exp2(-w)
            hi, low = split2(value)
            k_hi[j, here, :] = hi
            k_lo[j, here, :] = low
        return carry

    lax.fori_loop(0, cols, make_kernel, 0)

    await_all(irecv, i_r)
    got = devices * cap
    rep = jnp.where(iota((got, devices), 0) // cap == iota((got, devices), 1), 1.0, 0.0)
    seen = irecv[...].reshape(devices, 128)
    z_rows = mm(rep.astype(BF16), seen.astype(BF16))
    z_rows = jnp.where(iota((got, 128), 0) % cap == iota((got, 128), 1) // slots, z_rows, 0.0)
    by_slot = mm_nt(spread[:slots].astype(BF16), z_rows.astype(BF16))
    names = iota((st, got), 0).astype(F32)
    await_all(trecv, t_r)
    flat = trecv[...].reshape(got, slots * members).T
    rhs2 = jnp.zeros((2 * members, st), F32)
    for s in range(slots):
        hi, low = split2(flat[s * members : (s + 1) * members])
        hit = jnp.where(names == by_slot[s : s + 1], 1.0, 0.0).astype(BF16)
        rhs2 = rhs2 + mm_nt(jnp.concatenate([hi, low], axis=0), hit)
    rhs = rhs2[:members] + rhs2[members:]

    lane, sub = iota((members, 128), 1), iota((members, 128), 0)

    def operate(turn, v):
        vr, vc, sc = vrow.at[turn], vcol.at[turn], scal.at[turn]
        po, pi = pout.at[turn], pin.at[turn]
        vr[r] = v
        vc[c] = v
        to_row(lambda other, where: push(
            vr.at[r], vr.at[r], vr_s.at[turn], vr_r.at[turn], where))
        to_col(lambda other, where: push(
            vc.at[c], vc.at[c], vc_s.at[turn], vc_r.at[turn], where))

        def part(parts, k, here):
            hi, low = parts
            double = mm(jnp.concatenate([hi, low], axis=0), k_hi[k, here, :])
            return double[:members] + double[members:] + mm(hi, k_lo[k, here, :])

        mine = split2(v)
        for k in range(cols):
            base[k] = part(mine, k, pl.ds(0, st))
        await_all(vr, vr_r.at[turn])
        others = split2(jnp.concatenate([vr[row_of(k)] for k in range(1, rows)], axis=1))
        rest = pl.ds(st, (rows - 1) * st)
        for k in range(1, cols):
            total = base[k] + part(others, k, rest)
            base[k] = total
            po[around[k]] = total
            push(po.at[around[k]], pi.at[c], p_s.at[turn], p_r.at[turn], (r, around[k]))
        total = base[0] + part(others, 0, rest)
        pi[c] = total
        shift = nug[...] * v
        await_all(vc, vc_r.at[turn])
        acc = (total + shift) * v
        for k in range(1, cols):
            acc = acc + base[k] * vc[around[k]]
        norm = jnp.sum(v * v, axis=1, keepdims=True)
        product = jnp.sum(acc, axis=1, keepdims=True)
        line = jnp.where(lane == sub, norm, 0.0) + jnp.where(lane == sub + members, product, 0.0)
        sc[me] = jnp.sum(line, axis=0, keepdims=True)
        to_all(lambda other, where: push(
            sc.at[me], sc.at[me], s_s.at[turn], s_r.at[turn], where))
        await_all(pi, p_r.at[turn])
        image = shift + jnp.sum(pin[turn], axis=0)
        await_all(sc, s_r.at[turn])
        sums = jnp.sum(sc[...], axis=0)
        norm = jnp.sum(jnp.where(lane == sub, sums, 0.0), axis=1, keepdims=True)
        product = jnp.sum(jnp.where(lane == sub + members, sums, 0.0), axis=1, keepdims=True)
        return image, norm, product

    image, norm, product = operate(0, rhs)
    alpha = norm / product
    residual = rhs - alpha * image
    image_next, norm_next, product = operate(1, residual)
    ratio = norm_next / norm
    alpha_next = norm_next / (product - ratio * norm_next / alpha)
    out[0] = alpha * rhs + alpha_next * (residual + ratio * rhs)
    out[1] = residual - alpha_next * (image_next + ratio * image)

    await_all(zrow, zr_s)
    await_all(zcol, zc_s)
    await_all(tsend, t_s)
    await_all(isend, i_s)
    for turn in range(2):
        await_all(vrow.at[turn], vr_s.at[turn])
        await_all(vcol.at[turn], vc_s.at[turn])
        await_all(pout.at[turn], p_s.at[turn])
        await_all(scal.at[turn], s_s.at[turn])


def local(rows, cols, covariates, lengthscale, nugget, patch_values, patch_weights, block_index,
          slot_count, owner):
    devices = rows * cols
    feats, st = covariates.shape
    held, members, cells = patch_values.shape
    slots = patch_weights.shape[1]
    cap = max(128 // slots, 2 * held // devices)
    wide = -(-(6 * feats + 8) // 128) * 128
    dma = pltpu.SemaphoreType.DMA
    vmem = pltpu.VMEM
    scratch = [
        vmem((held * members, cells), patch_values.dtype),
        vmem((held * slots, cells), patch_weights.dtype),
        vmem((rows, feats, st), F32),
        vmem((cols, feats, st), F32),
        vmem((rows * st, wide), BF16),
        vmem((cols, wide, st), BF16),
        vmem((cols, rows * st, st), BF16),
        vmem((cols, rows * st, st), BF16),
        vmem((devices, cap, slots * members), F32),
        vmem((devices, cap, slots * members), F32),
        vmem((devices, 1, 128), F32),
        vmem((devices, 1, 128), F32),
        vmem((2, rows, members, st), F32),
        vmem((2, cols, members, st), F32),
        vmem((cols, members, st), F32),
        vmem((2, cols, members, st), F32),
        vmem((2, cols, members, st), F32),
        vmem((2, devices, 1, 128), F32),
    ]
    scratch += [dma((2,))] + [dma(())] * 8 + [dma((2,))] * 8
    spec = pl.BlockSpec(memory_space=pltpu.VMEM)
    far = pl.BlockSpec(memory_space=pl.ANY)
    both = pl.pallas_call(
        functools.partial(kernel, rows, cols, cap),
        out_shape=jax.ShapeDtypeStruct((2, members, st), F32),
        in_specs=[spec, spec, spec, far, far, spec, spec, spec],
        out_specs=spec,
        scratch_shapes=scratch,
        compiler_params=pltpu.CompilerParams(
            collective_id=0, has_side_effects=True, vmem_limit_bytes=56 * 2**20),
    )(
        covariates,
        lengthscale.reshape(1, feats),
        nugget.reshape(1, st),
        patch_values.reshape(held * members, cells),
        patch_weights.reshape(held * slots, cells),
        block_index.T,
        slot_count.reshape(1, held),
        owner.reshape(1, held),
    )
    return both[0], both[1]


def solution(mesh):
    placed = (
        P(None, ("row", "col")),
        P(),
        P(("row", "col")),
        P(("row", "col"), None, None),
        P(("row", "col"), None, None),
        P(("row", "col"), None),
        P(("row", "col")),
        P(("row", "col"), None),
    )
    return jax.shard_map(
        functools.partial(local, mesh.shape["row"], mesh.shape["col"]),
        mesh=mesh,
        in_specs=placed,
        out_specs=(P(None, ("row", "col")), P(None, ("row", "col"))),
        check_vma=False,
    )
```

```python
import functools
import math

import jax
import jax.numpy as jnp
from jax import lax
from jax.experimental import pallas as pl
from jax.experimental.pallas import tpu as pltpu
from jax.sharding import PartitionSpec as P

MESH = pl.DeviceIdType.MESH
F32, BF16 = jnp.float32, jnp.bfloat16
LOG2E = 1.0 / math.log(2.0)
SCALE = 5.0 * LOG2E * LOG2E
LINEAR = math.log(2.0)
SQUARE = math.log(2.0) ** 2 / 3.0


def iota(shape, axis):
    return lax.broadcasted_iota(jnp.int32, shape, axis)


def mm(a, b):
    return jnp.dot(a, b, preferred_element_type=F32)


def mm_nt(a, b):
    return lax.dot_general(a, b, (((1,), (1,)), ((), ())), preferred_element_type=F32)


def split2(x):
    hi = x.astype(BF16)
    return hi, (x - hi.astype(F32)).astype(BF16)


def split3(x):
    hi = x.astype(BF16).astype(F32)
    rest = x - hi
    mid = rest.astype(BF16).astype(F32)
    return hi, mid, rest - mid


def stack(parts, rows):
    place = iota((rows, parts[0].shape[1]), 0)
    out = jnp.zeros((rows, parts[0].shape[1]), F32)
    for number, part in enumerate(parts):
        out = jnp.where(place == number, part, out)
    return out


def features(z, left):
    feats, width = z.shape
    norm = split3(SCALE * jnp.sum(z * z, axis=0, keepdims=True))
    ones = [jnp.ones((1, width), F32)] * 3
    hi, mid, low = split3(z * (-2.0 * SCALE)) if left else split3(z)
    if left:
        parts, tail = [hi, hi, mid, mid, hi, low], list(norm) + ones
    else:
        parts, tail = [hi, mid, hi, mid, low, hi], ones + list(norm)
    used = 6 * feats + 8
    padded = -(-used // 128) * 128
    parts = parts + [stack(tail, 8)]
    if padded > used:
        parts.append(jnp.zeros((padded - used, width), F32))
    return jnp.concatenate(parts, axis=0)


def kernel(
    rows, cols, cap,
    cov, ls, nug, val_hbm, wts_hbm, idx, cnt, own,
    out,
    val, wts, zrow, zcol, left, right, k_hi, k_lo,
    tsend, trecv, isend, irecv, vrow, vcol, pout, pin, scal,
    load, zr_s, zr_r, zc_s, zc_r, t_s, t_r, i_s, i_r,
    vr_s, vr_r, vc_s, vc_r, p_s, p_r, s_s, s_r,
):
    devices = rows * cols
    r, c = lax.axis_index("row"), lax.axis_index("col")
    me = r * cols + c
    feats, st = cov.shape
    slots, held = idx.shape
    members = val.shape[0] // held
    group = 128 // slots

    def row_of(k):
        return jnp.where(r + k >= rows, r + k - rows, r + k)

    def col_of(k):
        return jnp.where(c + k >= cols, c + k - cols, c + k)

    around = [col_of(k) for k in range(cols)]

    def to_all(act):
        for k in range(1, cols):
            act(r * cols + around[k], (r, around[k]))

        def step(k, carry):
            other = row_of(k)
            for column in around:
                act(other * cols + column, (other, column))
            return carry

        lax.fori_loop(1, rows, step, 0)

    def to_row(act):
        for k in range(1, rows):
            act(row_of(k), (row_of(k), c))

    def to_col(act):
        for k in range(1, cols):
            act(around[k], (r, around[k]))

    def push(src, dst, ss, rs, where):
        pltpu.make_async_remote_copy(
            src_ref=src, dst_ref=dst, send_sem=ss, recv_sem=rs,
            device_id=where, device_id_type=MESH).start()

    def await_all(buf, sem):
        part = buf.at[pl.ds(0, buf.shape[0] - 1)]
        pltpu.make_async_copy(part, part, sem).wait()

    loads = [pltpu.make_async_copy(val_hbm, val, load.at[0]),
             pltpu.make_async_copy(wts_hbm, wts, load.at[1])]
    for copy in loads:
        copy.start()

    barrier = pltpu.get_barrier_semaphore()
    to_all(lambda other, where: pl.semaphore_signal(
        barrier, inc=1, device_id=where, device_id_type=MESH))

    diag = iota((feats, feats), 0) == iota((feats, feats), 1)
    scale = jnp.sum(jnp.where(diag, ls[...], 0.0), axis=1, keepdims=True)
    z = cov[...] / scale
    zrow[r] = z
    zcol[c] = z

    eye = iota((held, held), 0) == iota((held, held), 1)
    own_row = own[...].astype(F32)
    own_col = jnp.sum(jnp.where(eye, own_row, 0.0), axis=1, keepdims=True)
    same = (own_col == own_row) & (iota((held, held), 1) < iota((held, held), 0))
    rank = jnp.sum(jnp.where(same, 1.0, 0.0), axis=1, keepdims=True)
    position = own_col * cap + rank

    live = iota((slots, held), 0) < cnt[...]
    station = jnp.where(live, idx[...].astype(F32), float(st))
    station = jnp.concatenate([station, jnp.zeros((128 - slots, held), F32)], axis=0).T
    spread = jnp.where(iota((128, 128), 1) % slots == iota((128, 128), 0), 1.0, 0.0)
    wide = mm(station.astype(BF16), spread.astype(BF16))
    wide = jnp.where((iota((held, 128), 1) // slots).astype(F32) == rank, wide, 0.0)
    to_owner = jnp.where(iota((devices, held), 0).astype(F32) == own_row, 1.0, 0.0)
    index_rows = mm(to_owner.astype(BF16), wide.astype(BF16))
    for o in range(devices):
        isend[o] = index_rows[o : o + 1]
    irecv[me] = isend[me]

    pl.semaphore_wait(barrier, devices - 1)
    to_row(lambda other, where: push(zrow.at[r], zrow.at[r], zr_s, zr_r, where))
    to_col(lambda other, where: push(zcol.at[c], zcol.at[c], zc_s, zc_r, where))

    for copy in loads:
        copy.wait()
    blocks = iota((group, members, 128), 0) == iota((group, members, 128), 2) // slots
    lane_patch = iota((group, 128), 1) // slots == iota((group, 128), 0)
    slot_of = iota((members, 128), 1) % slots
    total = jnp.zeros((devices * cap, 2 * slots * members), F32)
    tables, spreads = [], []
    for g in range(held // group):
        cross = mm_nt(
            val[g * group * members : (g + 1) * group * members, :],
            wts[g * 128 : (g + 1) * 128, :],
        ).reshape(group, members, 128)
        terms = jnp.sum(jnp.where(blocks, cross, 0.0), axis=0)
        hi = terms.astype(BF16).astype(F32)
        low = terms - hi
        by_slot = [jnp.where(slot_of == s, part, 0.0) for part in (hi, low) for s in range(slots)]
        spreads.append(jnp.concatenate(by_slot, axis=0).astype(BF16))
        at = jnp.sum(
            jnp.where(lane_patch, position[g * group : (g + 1) * group], 0.0), axis=0, keepdims=True)
        tables.append(
            jnp.where(iota((devices * cap, 128), 0).astype(F32) == at, 1.0, 0.0).astype(BF16))
        if len(tables) == 4 or g + 1 == held // group:
            total = total + mm_nt(jnp.concatenate(tables, axis=1), jnp.concatenate(spreads, axis=1))
            tables, spreads = [], []
    packed = total[:, : slots * members] + total[:, slots * members :]
    tsend[...] = packed.reshape(devices, cap, slots * members)
    trecv[me] = tsend[me]

    def send_terms(other, where):
        push(tsend.at[other], trecv.at[me], t_s, t_r, where)
        push(isend.at[other], irecv.at[me], i_s, i_r, where)

    to_all(send_terms)

    await_all(zcol, zc_r)
    for k in range(cols):
        left[k * st : (k + 1) * st, :] = features(zcol[around[k]], True).T.astype(BF16)
    await_all(zrow, zr_r)
    for k in range(rows):
        right[k] = features(zrow[row_of(k)], False).astype(BF16)

    chunk = 2 * st
    chunks = cols * st // chunk

    def make_kernel(j, carry):
        for i in range(chunks):
            here = pl.ds(i * chunk, chunk)
            square = jnp.maximum(mm(left[here, :], right[j]), 1e-30)
            w = square * lax.rsqrt(square)
            value = (1.0 + LINEAR * w + SQUARE * square) * jnp.exp2(-w)
            hi, low = split2(value)
            k_hi[j, here, :] = hi
            k_lo[j, here, :] = low
        return carry

    lax.fori_loop(0, rows, make_kernel, 0)

    await_all(irecv, i_r)
    got = devices * cap
    rep = jnp.where(iota((got, devices), 0) // cap == iota((got, devices), 1), 1.0, 0.0)
    seen = irecv[...].reshape(devices, 128)
    z_rows = mm(rep.astype(BF16), seen.astype(BF16))
    z_rows = jnp.where(iota((got, 128), 0) % cap == iota((got, 128), 1) // slots, z_rows, 0.0)
    by_slot = mm_nt(spread[:slots].astype(BF16), z_rows.astype(BF16))
    names = iota((st, got), 0).astype(F32)
    await_all(trecv, t_r)
    flat = trecv[...].reshape(got, slots * members).T
    rhs2 = jnp.zeros((2 * members, st), F32)
    for s in range(slots):
        hi, low = split2(flat[s * members : (s + 1) * members])
        hit = jnp.where(names == by_slot[s : s + 1], 1.0, 0.0).astype(BF16)
        rhs2 = rhs2 + mm_nt(jnp.concatenate([hi, low], axis=0), hit)
    rhs = rhs2[:members] + rhs2[members:]

    lane, sub = iota((members, 128), 1), iota((members, 128), 0)

    def operate(turn, v):
        vr, vc, sc = vrow.at[turn], vcol.at[turn], scal.at[turn]
        po, pi = pout.at[turn], pin.at[turn]
        vr[r] = v
        vc[c] = v
        for k in range(1, cols):
            push(vc.at[c], vc.at[c], vc_s.at[turn], vc_r.at[turn, cols - k], (r, around[k]))
        to_row(lambda other, where: push(
            vr.at[r], vr.at[r], vr_s.at[turn], vr_r.at[turn], where))

        total = [jnp.zeros((members, st), F32)] * rows
        order = sorted(range(cols), key=lambda k: min(k, cols - k))
        for k in order:
            if k:
                part = vc.at[around[k]]
                pltpu.make_async_copy(part, part, vc_r.at[turn, k]).wait()
            block = vc[around[k]] if k else v
            hi, low = split2(block)
            both = jnp.concatenate([hi, low], axis=0)
            here = pl.ds(k * st, st)
            for j in range(rows):
                double = mm(both, k_hi[j, here, :])
                single = mm(hi, k_lo[j, here, :])
                total[j] = total[j] + (double[:members] + (double[members:] + single))
        for j in range(1, rows):
            other = row_of(j)
            po[other] = total[j]
            push(po.at[other], pi.at[r], p_s.at[turn], p_r.at[turn], (other, c))
        pi[r] = total[0]
        shift = nug[...] * v
        await_all(vr, vr_r.at[turn])
        acc = (total[0] + shift) * v
        for j in range(1, rows):
            acc = acc + total[j] * vr[row_of(j)]
        norm = jnp.sum(v * v, axis=1, keepdims=True)
        product = jnp.sum(acc, axis=1, keepdims=True)
        line = jnp.where(lane == sub, norm, 0.0) + jnp.where(lane == sub + members, product, 0.0)
        sc[me] = jnp.sum(line, axis=0, keepdims=True)
        to_all(lambda other, where: push(
            sc.at[me], sc.at[me], s_s.at[turn], s_r.at[turn], where))
        await_all(pi, p_r.at[turn])
        image = shift + jnp.sum(pin[turn], axis=0)
        await_all(sc, s_r.at[turn])
        sums = jnp.sum(sc[...], axis=0)
        norm = jnp.sum(jnp.where(lane == sub, sums, 0.0), axis=1, keepdims=True)
        product = jnp.sum(jnp.where(lane == sub + members, sums, 0.0), axis=1, keepdims=True)
        return image, norm, product

    image, norm, product = operate(0, rhs)
    alpha = norm / product
    residual = rhs - alpha * image
    image_next, norm_next, product = operate(1, residual)
    ratio = norm_next / norm
    alpha_next = norm_next / (product - ratio * norm_next / alpha)
    out[0] = alpha * rhs + alpha_next * (residual + ratio * rhs)
    out[1] = residual - alpha_next * (image_next + ratio * image)

    await_all(zrow, zr_s)
    await_all(zcol, zc_s)
    await_all(tsend, t_s)
    await_all(isend, i_s)
    for turn in range(2):
        await_all(vrow.at[turn], vr_s.at[turn])
        await_all(vcol.at[turn], vc_s.at[turn])
        await_all(pout.at[turn], p_s.at[turn])
        await_all(scal.at[turn], s_s.at[turn])


def local(rows, cols, covariates, lengthscale, nugget, patch_values, patch_weights, block_index,
          slot_count, owner):
    devices = rows * cols
    feats, st = covariates.shape
    held, members, cells = patch_values.shape
    slots = patch_weights.shape[1]
    cap = max(128 // slots, 2 * held // devices)
    wide = -(-(6 * feats + 8) // 128) * 128
    dma = pltpu.SemaphoreType.DMA
    vmem = pltpu.VMEM
    scratch = [
        vmem((held * members, cells), patch_values.dtype),
        vmem((held * slots, cells), patch_weights.dtype),
        vmem((rows, feats, st), F32),
        vmem((cols, feats, st), F32),
        vmem((cols * st, wide), BF16),
        vmem((rows, wide, st), BF16),
        vmem((rows, cols * st, st), BF16),
        vmem((rows, cols * st, st), BF16),
        vmem((devices, cap, slots * members), F32),
        vmem((devices, cap, slots * members), F32),
        vmem((devices, 1, 128), F32),
        vmem((devices, 1, 128), F32),
        vmem((2, rows, members, st), F32),
        vmem((2, cols, members, st), F32),
        vmem((2, rows, members, st), F32),
        vmem((2, rows, members, st), F32),
        vmem((2, devices, 1, 128), F32),
    ]
    scratch += [dma((2,))] + [dma(())] * 8 + [dma((2,))] * 3 + [dma((2, cols))] + [dma((2,))] * 4
    spec = pl.BlockSpec(memory_space=pltpu.VMEM)
    far = pl.BlockSpec(memory_space=pl.ANY)
    both = pl.pallas_call(
        functools.partial(kernel, rows, cols, cap),
        out_shape=jax.ShapeDtypeStruct((2, members, st), F32),
        in_specs=[spec, spec, spec, far, far, spec, spec, spec],
        out_specs=spec,
        scratch_shapes=scratch,
        compiler_params=pltpu.CompilerParams(
            collective_id=0, has_side_effects=True, vmem_limit_bytes=56 * 2**20),
    )(
        covariates,
        lengthscale.reshape(1, feats),
        nugget.reshape(1, st),
        patch_values.reshape(held * members, cells),
        patch_weights.reshape(held * slots, cells),
        block_index.T,
        slot_count.reshape(1, held),
        owner.reshape(1, held),
    )
    return both[0], both[1]


def solution(mesh):
    placed = (
        P(None, ("row", "col")),
        P(),
        P(("row", "col")),
        P(("row", "col"), None, None),
        P(("row", "col"), None, None),
        P(("row", "col"), None),
        P(("row", "col")),
        P(("row", "col"), None),
    )
    return jax.shard_map(
        functools.partial(local, mesh.shape["row"], mesh.shape["col"]),
        mesh=mesh,
        in_specs=placed,
        out_specs=(P(None, ("row", "col")), P(None, ("row", "col"))),
        check_vma=False,
    )
```

```python
import functools
import math

import jax
import jax.numpy as jnp
from jax import lax
from jax.experimental import pallas as pl
from jax.experimental.pallas import tpu as pltpu
from jax.sharding import PartitionSpec as P

MESH = pl.DeviceIdType.MESH
F32, BF16 = jnp.float32, jnp.bfloat16
LOG2E = 1.0 / math.log(2.0)
SCALE = 5.0 * LOG2E * LOG2E
LINEAR = math.log(2.0)
SQUARE = math.log(2.0) ** 2 / 3.0


def iota(shape, axis):
    return lax.broadcasted_iota(jnp.int32, shape, axis)


def mm(a, b):
    return jnp.dot(a, b, preferred_element_type=F32)


def mm_nt(a, b):
    return lax.dot_general(a, b, (((1,), (1,)), ((), ())), preferred_element_type=F32)


def split2(x):
    hi = x.astype(BF16)
    return hi, (x - hi.astype(F32)).astype(BF16)


def split3(x):
    hi = x.astype(BF16).astype(F32)
    rest = x - hi
    mid = rest.astype(BF16).astype(F32)
    return hi, mid, rest - mid


def stack(parts, rows):
    place = iota((rows, parts[0].shape[1]), 0)
    out = jnp.zeros((rows, parts[0].shape[1]), F32)
    for number, part in enumerate(parts):
        out = jnp.where(place == number, part, out)
    return out


def features(z, left):
    feats, width = z.shape
    norm = split3(SCALE * jnp.sum(z * z, axis=0, keepdims=True))
    ones = [jnp.ones((1, width), F32)] * 3
    hi, mid, low = split3(z * (-2.0 * SCALE)) if left else split3(z)
    if left:
        parts, tail = [hi, hi, mid, mid, hi, low], list(norm) + ones
    else:
        parts, tail = [hi, mid, hi, mid, low, hi], ones + list(norm)
    used = 6 * feats + 8
    padded = -(-used // 128) * 128
    parts = parts + [stack(tail, 8)]
    if padded > used:
        parts.append(jnp.zeros((padded - used, width), F32))
    return jnp.concatenate(parts, axis=0)


def kernel(
    rows, cols, cap,
    cov, ls, nug, val_hbm, wts_hbm, idx, cnt, own,
    out,
    val, wts, zrow, zcol, left, right, k_hi, k_lo,
    tsend, trecv, isend, irecv, vrow, vcol, base, pout, pin, scal,
    load, zr_s, zr_r, zc_s, zc_r, t_s, t_r, i_s, i_r,
    vr_s, vr_r, vc_s, vc_r, p_s, p_r, s_s, s_r,
):
    devices = rows * cols
    r, c = lax.axis_index("row"), lax.axis_index("col")
    me = r * cols + c
    feats, st = cov.shape
    slots, held = idx.shape
    members = val.shape[0] // held
    group = 128 // slots

    def row_of(k):
        return jnp.where(r + k >= rows, r + k - rows, r + k)

    def col_of(k):
        return jnp.where(c + k >= cols, c + k - cols, c + k)

    around = [col_of(k) for k in range(cols)]

    def to_all(act):
        for k in range(1, cols):
            act(r * cols + around[k], (r, around[k]))

        def step(k, carry):
            other = row_of(k)
            for column in around:
                act(other * cols + column, (other, column))
            return carry

        lax.fori_loop(1, rows, step, 0)

    def to_row(act):
        for k in range(1, rows):
            act(row_of(k), (row_of(k), c))

    def to_col(act):
        for k in range(1, cols):
            act(around[k], (r, around[k]))

    def push(src, dst, ss, rs, where):
        pltpu.make_async_remote_copy(
            src_ref=src, dst_ref=dst, send_sem=ss, recv_sem=rs,
            device_id=where, device_id_type=MESH).start()

    def await_all(buf, sem):
        part = buf.at[pl.ds(0, buf.shape[0] - 1)]
        pltpu.make_async_copy(part, part, sem).wait()

    loads = [pltpu.make_async_copy(val_hbm, val, load.at[0]),
             pltpu.make_async_copy(wts_hbm, wts, load.at[1])]
    for copy in loads:
        copy.start()

    barrier = pltpu.get_barrier_semaphore()
    to_all(lambda other, where: pl.semaphore_signal(
        barrier, inc=1, device_id=where, device_id_type=MESH))

    diag = iota((feats, feats), 0) == iota((feats, feats), 1)
    scale = jnp.sum(jnp.where(diag, ls[...], 0.0), axis=1, keepdims=True)
    z = cov[...] / scale
    zrow[r] = z
    zcol[c] = z

    eye = iota((held, held), 0) == iota((held, held), 1)
    own_row = own[...].astype(F32)
    own_col = jnp.sum(jnp.where(eye, own_row, 0.0), axis=1, keepdims=True)
    same = (own_col == own_row) & (iota((held, held), 1) < iota((held, held), 0))
    rank = jnp.sum(jnp.where(same, 1.0, 0.0), axis=1, keepdims=True)
    position = own_col * cap + rank

    live = iota((slots, held), 0) < cnt[...]
    station = jnp.where(live, idx[...].astype(F32), float(st))
    station = jnp.concatenate([station, jnp.zeros((128 - slots, held), F32)], axis=0).T
    spread = jnp.where(iota((128, 128), 1) % slots == iota((128, 128), 0), 1.0, 0.0)
    wide = mm(station.astype(BF16), spread.astype(BF16))
    wide = jnp.where((iota((held, 128), 1) // slots).astype(F32) == rank, wide, 0.0)
    to_owner = jnp.where(iota((devices, held), 0).astype(F32) == own_row, 1.0, 0.0)
    index_rows = mm(to_owner.astype(BF16), wide.astype(BF16))
    for o in range(devices):
        isend[o] = index_rows[o : o + 1]
    irecv[me] = isend[me]

    pl.semaphore_wait(barrier, devices - 1)
    to_row(lambda other, where: push(zrow.at[r], zrow.at[r], zr_s, zr_r, where))
    to_col(lambda other, where: push(zcol.at[c], zcol.at[c], zc_s, zc_r, where))

    for copy in loads:
        copy.wait()
    blocks = iota((group, members, 128), 0) == iota((group, members, 128), 2) // slots
    lane_patch = iota((group, 128), 1) // slots == iota((group, 128), 0)
    slot_of = iota((members, 128), 1) % slots
    tables, spreads = [], []
    for g in range(held // group):
        cross = mm_nt(
            val[g * group * members : (g + 1) * group * members, :],
            wts[g * 128 : (g + 1) * 128, :],
        ).reshape(group, members, 128)
        terms = jnp.sum(jnp.where(blocks, cross, 0.0), axis=0)
        hi = terms.astype(BF16).astype(F32)
        low = terms - hi
        by_slot = [jnp.where(slot_of == s, part, 0.0) for part in (hi, low) for s in range(slots)]
        spreads.append(jnp.concatenate(by_slot, axis=0).astype(BF16))
        at = jnp.sum(
            jnp.where(lane_patch, position[g * group : (g + 1) * group], 0.0), axis=0, keepdims=True)
        tables.append(
            jnp.where(iota((devices * cap, 128), 0).astype(F32) == at, 1.0, 0.0).astype(BF16))
    total = mm_nt(jnp.concatenate(tables, axis=1), jnp.concatenate(spreads, axis=1))
    packed = total[:, : slots * members] + total[:, slots * members :]
    tsend[...] = packed.reshape(devices, cap, slots * members)
    trecv[me] = tsend[me]

    def send_terms(other, where):
        push(tsend.at[other], trecv.at[me], t_s, t_r, where)
        push(isend.at[other], irecv.at[me], i_s, i_r, where)

    to_all(send_terms)

    await_all(zrow, zr_r)
    for k in range(rows):
        left[k * st : (k + 1) * st, :] = features(zrow[row_of(k)], True).T.astype(BF16)
    await_all(zcol, zc_r)

    for k in range(cols):
        right[k] = features(zcol[around[k]], False).astype(BF16)

    chunk = 2 * st
    chunks = rows * st // chunk

    def make_kernel(pair, carry):
        for t in range(2 * chunks):
            j, here = 2 * pair + t // chunks, pl.ds(t % chunks * chunk, chunk)
            square = jnp.maximum(mm(left[here, :], right[j]), 1e-30)
            w = square * lax.rsqrt(square)
            value = (1.0 + LINEAR * w + SQUARE * square) * jnp.exp2(-w)
            hi, low = split2(value)
            k_hi[j, here, :] = hi
            k_lo[j, here, :] = low
        return carry

    lax.fori_loop(0, cols // 2, make_kernel, 0)

    await_all(irecv, i_r)
    got = devices * cap
    rep = jnp.where(iota((got, devices), 0) // cap == iota((got, devices), 1), 1.0, 0.0)
    seen = irecv[...].reshape(devices, 128)
    z_rows = mm(rep.astype(BF16), seen.astype(BF16))
    z_rows = jnp.where(iota((got, 128), 0) % cap == iota((got, 128), 1) // slots, z_rows, 0.0)
    by_slot = mm_nt(spread[:slots].astype(BF16), z_rows.astype(BF16))
    names = iota((st, got), 0).astype(F32)
    await_all(trecv, t_r)
    flat = trecv[...].reshape(got, slots * members).T
    rhs2 = jnp.zeros((2 * members, st), F32)
    for s in range(slots):
        hi, low = split2(flat[s * members : (s + 1) * members])
        hit = jnp.where(names == by_slot[s : s + 1], 1.0, 0.0).astype(BF16)
        rhs2 = rhs2 + mm_nt(jnp.concatenate([hi, low], axis=0), hit)
    rhs = rhs2[:members] + rhs2[members:]

    lane, sub = iota((members, 128), 1), iota((members, 128), 0)

    def operate(turn, v):
        vr, vc, sc = vrow.at[turn], vcol.at[turn], scal.at[turn]
        po, pi = pout.at[turn], pin.at[turn]
        vr[r] = v
        vc[c] = v
        to_row(lambda other, where: push(
            vr.at[r], vr.at[r], vr_s.at[turn], vr_r.at[turn], where))
        to_col(lambda other, where: push(
            vc.at[c], vc.at[c], vc_s.at[turn], vc_r.at[turn], where))

        def part(parts, k, here):
            hi, low = parts
            double = mm(jnp.concatenate([hi, low], axis=0), k_hi[k, here, :])
            return double[:members] + double[members:] + mm(hi, k_lo[k, here, :])

        mine = split2(v)
        for k in range(cols):
            base[k] = part(mine, k, pl.ds(0, st))
        await_all(vr, vr_r.at[turn])
        others = split2(jnp.concatenate([vr[row_of(k)] for k in range(1, rows)], axis=1))
        rest = pl.ds(st, (rows - 1) * st)
        for k in sorted(range(1, cols), key=lambda k: -min(k, cols - k)):
            total = base[k] + part(others, k, rest)
            base[k] = total
            po[around[k]] = total
            push(po.at[around[k]], pi.at[c], p_s.at[turn], p_r.at[turn], (r, around[k]))
        total = base[0] + part(others, 0, rest)
        pi[c] = total
        shift = nug[...] * v
        await_all(vc, vc_r.at[turn])
        acc = (total + shift) * v
        for k in range(1, cols):
            acc = acc + base[k] * vc[around[k]]
        norm = jnp.sum(v * v, axis=1, keepdims=True)
        product = jnp.sum(acc, axis=1, keepdims=True)
        line = jnp.where(lane == sub, norm, 0.0) + jnp.where(lane == sub + members, product, 0.0)
        sc[me] = jnp.sum(line, axis=0, keepdims=True)
        to_all(lambda other, where: push(
            sc.at[me], sc.at[me], s_s.at[turn], s_r.at[turn], where))
        await_all(pi, p_r.at[turn])
        image = shift + jnp.sum(pin[turn], axis=0)
        await_all(sc, s_r.at[turn])
        sums = jnp.sum(sc[...], axis=0)
        norm = jnp.sum(jnp.where(lane == sub, sums, 0.0), axis=1, keepdims=True)
        product = jnp.sum(jnp.where(lane == sub + members, sums, 0.0), axis=1, keepdims=True)
        return image, norm, product

    image, norm, product = operate(0, rhs)
    alpha = norm / product
    residual = rhs - alpha * image
    image_next, norm_next, product = operate(1, residual)
    ratio = norm_next / norm
    alpha_next = norm_next / (product - ratio * norm_next / alpha)
    out[0] = alpha * rhs + alpha_next * (residual + ratio * rhs)
    out[1] = residual - alpha_next * (image_next + ratio * image)

    await_all(zrow, zr_s)
    await_all(zcol, zc_s)
    await_all(tsend, t_s)
    await_all(isend, i_s)
    for turn in range(2):
        await_all(vrow.at[turn], vr_s.at[turn])
        await_all(vcol.at[turn], vc_s.at[turn])
        await_all(pout.at[turn], p_s.at[turn])
        await_all(scal.at[turn], s_s.at[turn])


def local(rows, cols, covariates, lengthscale, nugget, patch_values, patch_weights, block_index,
          slot_count, owner):
    devices = rows * cols
    feats, st = covariates.shape
    held, members, cells = patch_values.shape
    slots = patch_weights.shape[1]
    cap = max(128 // slots, 2 * held // devices)
    wide = -(-(6 * feats + 8) // 128) * 128
    dma = pltpu.SemaphoreType.DMA
    vmem = pltpu.VMEM
    scratch = [
        vmem((held * members, cells), patch_values.dtype),
        vmem((held * slots, cells), patch_weights.dtype),
        vmem((rows, feats, st), F32),
        vmem((cols, feats, st), F32),
        vmem((rows * st, wide), BF16),
        vmem((cols, wide, st), BF16),
        vmem((cols, rows * st, st), BF16),
        vmem((cols, rows * st, st), BF16),
        vmem((devices, cap, slots * members), F32),
        vmem((devices, cap, slots * members), F32),
        vmem((devices, 1, 128), F32),
        vmem((devices, 1, 128), F32),
        vmem((2, rows, members, st), F32),
        vmem((2, cols, members, st), F32),
        vmem((cols, members, st), F32),
        vmem((2, cols, members, st), F32),
        vmem((2, cols, members, st), F32),
        vmem((2, devices, 1, 128), F32),
    ]
    scratch += [dma((2,))] + [dma(())] * 8 + [dma((2,))] * 8
    spec = pl.BlockSpec(memory_space=pltpu.VMEM)
    far = pl.BlockSpec(memory_space=pl.ANY)
    both = pl.pallas_call(
        functools.partial(kernel, rows, cols, cap),
        out_shape=jax.ShapeDtypeStruct((2, members, st), F32),
        in_specs=[spec, spec, spec, far, far, spec, spec, spec],
        out_specs=spec,
        scratch_shapes=scratch,
        compiler_params=pltpu.CompilerParams(
            collective_id=0, has_side_effects=True, vmem_limit_bytes=56 * 2**20),
    )(
        covariates,
        lengthscale.reshape(1, feats),
        nugget.reshape(1, st),
        patch_values.reshape(held * members, cells),
        patch_weights.reshape(held * slots, cells),
        block_index.T,
        slot_count.reshape(1, held),
        owner.reshape(1, held),
    )
    return both[0], both[1]


def solution(mesh):
    placed = (
        P(None, ("row", "col")),
        P(),
        P(("row", "col")),
        P(("row", "col"), None, None),
        P(("row", "col"), None, None),
        P(("row", "col"), None),
        P(("row", "col")),
        P(("row", "col"), None),
    )
    return jax.shard_map(
        functools.partial(local, mesh.shape["row"], mesh.shape["col"]),
        mesh=mesh,
        in_specs=placed,
        out_specs=(P(None, ("row", "col")), P(None, ("row", "col"))),
        check_vma=False,
    )
```

```python
import functools
import math

import jax
import jax.numpy as jnp
from jax import lax
from jax.experimental import pallas as pl
from jax.experimental.pallas import tpu as pltpu
from jax.sharding import PartitionSpec as P

MESH = pl.DeviceIdType.MESH
F32, BF16 = jnp.float32, jnp.bfloat16
LOG2E = 1.0 / math.log(2.0)
SCALE = 5.0 * LOG2E * LOG2E
LINEAR = math.log(2.0)
SQUARE = math.log(2.0) ** 2 / 3.0


def iota(shape, axis):
    return lax.broadcasted_iota(jnp.int32, shape, axis)


def mm(a, b):
    return jnp.dot(a, b, preferred_element_type=F32)


def mm_nt(a, b):
    return lax.dot_general(a, b, (((1,), (1,)), ((), ())), preferred_element_type=F32)


def split2(x):
    hi = x.astype(BF16)
    return hi, (x - hi.astype(F32)).astype(BF16)


def split3(x):
    hi = x.astype(BF16).astype(F32)
    rest = x - hi
    mid = rest.astype(BF16).astype(F32)
    return hi, mid, rest - mid


def stack(parts, rows):
    place = iota((rows, parts[0].shape[1]), 0)
    out = jnp.zeros((rows, parts[0].shape[1]), F32)
    for number, part in enumerate(parts):
        out = jnp.where(place == number, part, out)
    return out


def features(z, left):
    feats, width = z.shape
    norm = split3(SCALE * jnp.sum(z * z, axis=0, keepdims=True))
    ones = [jnp.ones((1, width), F32)] * 3
    hi, mid, low = split3(z * (-2.0 * SCALE)) if left else split3(z)
    if left:
        parts, tail = [hi, hi, mid, mid, hi, low], list(norm) + ones
    else:
        parts, tail = [hi, mid, hi, mid, low, hi], ones + list(norm)
    used = 6 * feats + 8
    padded = -(-used // 128) * 128
    parts = parts + [stack(tail, 8)]
    if padded > used:
        parts.append(jnp.zeros((padded - used, width), F32))
    return jnp.concatenate(parts, axis=0)


def kernel(
    rows, cols, cap,
    cov, ls, nug, val_hbm, wts_hbm, idx, cnt, own,
    out,
    val, wts, zrow, zcol, left, right, k_hi, k_lo,
    tsend, trecv, isend, irecv, vrow, vcol, base, pout, pin, scal,
    load, zr_s, zr_r, zc_s, zc_r, t_s, t_r, i_s, i_r,
    vr_s, vr_r, vc_s, vc_r, p_s, p_r, s_s, s_r,
):
    devices = rows * cols
    r, c = lax.axis_index("row"), lax.axis_index("col")
    me = r * cols + c
    feats, st = cov.shape
    slots, held = idx.shape
    members = val.shape[0] // held
    group = 128 // slots

    def row_of(k):
        return jnp.where(r + k >= rows, r + k - rows, r + k)

    def col_of(k):
        return jnp.where(c + k >= cols, c + k - cols, c + k)

    around = [col_of(k) for k in range(cols)]

    def to_all(act):
        for k in range(1, cols):
            act(r * cols + around[k], (r, around[k]))

        def step(k, carry):
            other = row_of(k)
            for column in around:
                act(other * cols + column, (other, column))
            return carry

        lax.fori_loop(1, rows, step, 0)

    def to_row(act):
        for k in range(1, rows):
            act(row_of(k), (row_of(k), c))

    def to_col(act):
        for k in range(1, cols):
            act(around[k], (r, around[k]))

    def push(src, dst, ss, rs, where):
        pltpu.make_async_remote_copy(
            src_ref=src, dst_ref=dst, send_sem=ss, recv_sem=rs,
            device_id=where, device_id_type=MESH).start()

    def await_all(buf, sem):
        part = buf.at[pl.ds(0, buf.shape[0] - 1)]
        pltpu.make_async_copy(part, part, sem).wait()

    loads = [pltpu.make_async_copy(val_hbm, val, load.at[0]),
             pltpu.make_async_copy(wts_hbm, wts, load.at[1])]
    for copy in loads:
        copy.start()

    barrier = pltpu.get_barrier_semaphore()
    to_all(lambda other, where: pl.semaphore_signal(
        barrier, inc=1, device_id=where, device_id_type=MESH))

    diag = iota((feats, feats), 0) == iota((feats, feats), 1)
    scale = jnp.sum(jnp.where(diag, ls[...], 0.0), axis=1, keepdims=True)
    z = cov[...] / scale
    zrow[r] = z
    zcol[c] = z

    eye = iota((held, held), 0) == iota((held, held), 1)
    own_row = own[...].astype(F32)
    own_col = jnp.sum(jnp.where(eye, own_row, 0.0), axis=1, keepdims=True)
    same = (own_col == own_row) & (iota((held, held), 1) < iota((held, held), 0))
    rank = jnp.sum(jnp.where(same, 1.0, 0.0), axis=1, keepdims=True)
    position = own_col * cap + rank

    live = iota((slots, held), 0) < cnt[...]
    station = jnp.where(live, idx[...].astype(F32), float(st))
    station = jnp.concatenate([station, jnp.zeros((128 - slots, held), F32)], axis=0).T
    spread = jnp.where(iota((128, 128), 1) % slots == iota((128, 128), 0), 1.0, 0.0)
    wide = mm(station.astype(BF16), spread.astype(BF16))
    wide = jnp.where((iota((held, 128), 1) // slots).astype(F32) == rank, wide, 0.0)
    to_owner = jnp.where(iota((devices, held), 0).astype(F32) == own_row, 1.0, 0.0)
    index_rows = mm(to_owner.astype(BF16), wide.astype(BF16))
    for o in range(devices):
        isend[o] = index_rows[o : o + 1]
    irecv[me] = isend[me]

    pl.semaphore_wait(barrier, devices - 1)
    to_row(lambda other, where: push(zrow.at[r], zrow.at[r], zr_s, zr_r, where))
    to_col(lambda other, where: push(zcol.at[c], zcol.at[c], zc_s, zc_r, where))

    to_all(lambda other, where: push(isend.at[other], irecv.at[me], i_s, i_r, where))

    for copy in loads:
        copy.wait()
    blocks = iota((group, members, 128), 0) == iota((group, members, 128), 2) // slots
    lane_patch = iota((group, 128), 1) // slots == iota((group, 128), 0)
    slot_of = iota((members, 128), 1) % slots
    total = jnp.zeros((devices * cap, 2 * slots * members), F32)
    tables, spreads = [], []
    for g in range(held // group):
        cross = mm_nt(
            val[g * group * members : (g + 1) * group * members, :],
            wts[g * 128 : (g + 1) * 128, :],
        ).reshape(group, members, 128)
        terms = jnp.sum(jnp.where(blocks, cross, 0.0), axis=0)
        hi = terms.astype(BF16).astype(F32)
        low = terms - hi
        by_slot = [jnp.where(slot_of == s, part, 0.0) for part in (hi, low) for s in range(slots)]
        spreads.append(jnp.concatenate(by_slot, axis=0).astype(BF16))
        at = jnp.sum(
            jnp.where(lane_patch, position[g * group : (g + 1) * group], 0.0), axis=0, keepdims=True)
        tables.append(
            jnp.where(iota((devices * cap, 128), 0).astype(F32) == at, 1.0, 0.0).astype(BF16))
        if len(tables) == 4 or g + 1 == held // group:
            total = total + mm_nt(jnp.concatenate(tables, axis=1), jnp.concatenate(spreads, axis=1))
            tables, spreads = [], []
    packed = total[:, : slots * members] + total[:, slots * members :]
    tsend[...] = packed.reshape(devices, cap, slots * members)
    trecv[me] = tsend[me]

    def send_terms(other, where):
        push(tsend.at[other], trecv.at[me], t_s, t_r, where)

    to_all(send_terms)

    await_all(zrow, zr_r)
    for k in range(rows):
        left[k * st : (k + 1) * st, :] = features(zrow[row_of(k)], True).T.astype(BF16)
    await_all(zcol, zc_r)

    def make_right(k, carry):
        right[k] = features(zcol[col_of(k)], False).astype(BF16)
        return carry

    lax.fori_loop(0, cols, make_right, 0)

    chunk = 2 * st
    chunks = rows * st // chunk

    def make_kernel(j, carry):
        for i in range(chunks):
            here = pl.ds(i * chunk, chunk)
            square = jnp.maximum(mm(left[here, :], right[j]), 1e-30)
            w = square * lax.rsqrt(square)
            value = (1.0 + LINEAR * w + SQUARE * square) * jnp.exp2(-w)
            hi, low = split2(value)
            k_hi[j, here, :] = hi
            k_lo[j, here, :] = low
        return carry

    lax.fori_loop(0, cols, make_kernel, 0)

    await_all(irecv, i_r)
    got = devices * cap
    rep = jnp.where(iota((got, devices), 0) // cap == iota((got, devices), 1), 1.0, 0.0)
    seen = irecv[...].reshape(devices, 128)
    z_rows = mm(rep.astype(BF16), seen.astype(BF16))
    z_rows = jnp.where(iota((got, 128), 0) % cap == iota((got, 128), 1) // slots, z_rows, 0.0)
    by_slot = mm_nt(spread[:slots].astype(BF16), z_rows.astype(BF16))
    names = iota((st, got), 0).astype(F32)
    await_all(trecv, t_r)
    flat = trecv[...].reshape(got, slots * members).T
    rhs2 = jnp.zeros((2 * members, st), F32)
    for s in range(slots):
        hi, low = split2(flat[s * members : (s + 1) * members])
        hit = jnp.where(names == by_slot[s : s + 1], 1.0, 0.0).astype(BF16)
        rhs2 = rhs2 + mm_nt(jnp.concatenate([hi, low], axis=0), hit)
    rhs = rhs2[:members] + rhs2[members:]

    lane, sub = iota((members, 128), 1), iota((members, 128), 0)

    def operate(turn, v):
        vr, vc, sc = vrow.at[turn], vcol.at[turn], scal.at[turn]
        po, pi = pout.at[turn], pin.at[turn]
        vr[r] = v
        vc[c] = v
        to_row(lambda other, where: push(
            vr.at[r], vr.at[r], vr_s.at[turn], vr_r.at[turn], where))
        to_col(lambda other, where: push(
            vc.at[c], vc.at[c], vc_s.at[turn], vc_r.at[turn], where))

        def part(parts, k, here):
            hi, low = parts
            double = mm(jnp.concatenate([hi, low], axis=0), k_hi[k, here, :])
            return double[:members] + double[members:] + mm(hi, k_lo[k, here, :])

        mine = split2(v)
        for k in range(cols):
            base[k] = part(mine, k, pl.ds(0, st))
        await_all(vr, vr_r.at[turn])
        others = split2(jnp.concatenate([vr[row_of(k)] for k in range(1, rows)], axis=1))
        rest = pl.ds(st, (rows - 1) * st)
        for k in range(1, cols):
            total = base[k] + part(others, k, rest)
            base[k] = total
            po[around[k]] = total
            push(po.at[around[k]], pi.at[c], p_s.at[turn], p_r.at[turn], (r, around[k]))
        total = base[0] + part(others, 0, rest)
        pi[c] = total
        shift = nug[...] * v
        await_all(vc, vc_r.at[turn])
        acc = (total + shift) * v
        for k in range(1, cols):
            acc = acc + base[k] * vc[around[k]]
        norm = jnp.sum(v * v, axis=1, keepdims=True)
        product = jnp.sum(acc, axis=1, keepdims=True)
        line = jnp.where(lane == sub, norm, 0.0) + jnp.where(lane == sub + members, product, 0.0)
        sc[me] = jnp.sum(line, axis=0, keepdims=True)
        to_all(lambda other, where: push(
            sc.at[me], sc.at[me], s_s.at[turn], s_r.at[turn], where))
        await_all(pi, p_r.at[turn])
        image = shift + jnp.sum(pin[turn], axis=0)
        await_all(sc, s_r.at[turn])
        sums = jnp.sum(sc[...], axis=0)
        norm = jnp.sum(jnp.where(lane == sub, sums, 0.0), axis=1, keepdims=True)
        product = jnp.sum(jnp.where(lane == sub + members, sums, 0.0), axis=1, keepdims=True)
        return image, norm, product

    image, norm, product = operate(0, rhs)
    alpha = norm / product
    residual = rhs - alpha * image
    image_next, norm_next, product = operate(1, residual)
    ratio = norm_next / norm
    alpha_next = norm_next / (product - ratio * norm_next / alpha)
    out[0] = alpha * rhs + alpha_next * (residual + ratio * rhs)
    out[1] = residual - alpha_next * (image_next + ratio * image)

    await_all(zrow, zr_s)
    await_all(zcol, zc_s)
    await_all(tsend, t_s)
    await_all(isend, i_s)
    for turn in range(2):
        await_all(vrow.at[turn], vr_s.at[turn])
        await_all(vcol.at[turn], vc_s.at[turn])
        await_all(pout.at[turn], p_s.at[turn])
        await_all(scal.at[turn], s_s.at[turn])


def local(rows, cols, covariates, lengthscale, nugget, patch_values, patch_weights, block_index,
          slot_count, owner):
    devices = rows * cols
    feats, st = covariates.shape
    held, members, cells = patch_values.shape
    slots = patch_weights.shape[1]
    cap = max(128 // slots, 2 * held // devices)
    wide = -(-(6 * feats + 8) // 128) * 128
    dma = pltpu.SemaphoreType.DMA
    vmem = pltpu.VMEM
    scratch = [
        vmem((held * members, cells), patch_values.dtype),
        vmem((held * slots, cells), patch_weights.dtype),
        vmem((rows, feats, st), F32),
        vmem((cols, feats, st), F32),
        vmem((rows * st, wide), BF16),
        vmem((cols, wide, st), BF16),
        vmem((cols, rows * st, st), BF16),
        vmem((cols, rows * st, st), BF16),
        vmem((devices, cap, slots * members), F32),
        vmem((devices, cap, slots * members), F32),
        vmem((devices, 1, 128), F32),
        vmem((devices, 1, 128), F32),
        vmem((2, rows, members, st), F32),
        vmem((2, cols, members, st), F32),
        vmem((cols, members, st), F32),
        vmem((2, cols, members, st), F32),
        vmem((2, cols, members, st), F32),
        vmem((2, devices, 1, 128), F32),
    ]
    scratch += [dma((2,))] + [dma(())] * 8 + [dma((2,))] * 8
    spec = pl.BlockSpec(memory_space=pltpu.VMEM)
    far = pl.BlockSpec(memory_space=pl.ANY)
    both = pl.pallas_call(
        functools.partial(kernel, rows, cols, cap),
        out_shape=jax.ShapeDtypeStruct((2, members, st), F32),
        in_specs=[spec, spec, spec, far, far, spec, spec, spec],
        out_specs=spec,
        scratch_shapes=scratch,
        compiler_params=pltpu.CompilerParams(
            collective_id=0, has_side_effects=True, vmem_limit_bytes=56 * 2**20),
    )(
        covariates,
        lengthscale.reshape(1, feats),
        nugget.reshape(1, st),
        patch_values.reshape(held * members, cells),
        patch_weights.reshape(held * slots, cells),
        block_index.T,
        slot_count.reshape(1, held),
        owner.reshape(1, held),
    )
    return both[0], both[1]


def solution(mesh):
    placed = (
        P(None, ("row", "col")),
        P(),
        P(("row", "col")),
        P(("row", "col"), None, None),
        P(("row", "col"), None, None),
        P(("row", "col"), None),
        P(("row", "col")),
        P(("row", "col"), None),
    )
    return jax.shard_map(
        functools.partial(local, mesh.shape["row"], mesh.shape["col"]),
        mesh=mesh,
        in_specs=placed,
        out_specs=(P(None, ("row", "col")), P(None, ("row", "col"))),
        check_vma=False,
    )
```
